1024 devices in a mesh: expert: 32 (over z), dp: 32 (over x, y, core).
Axes of the slice: x: 4, y: 4, z: 32, core: 2. Of those that a mesh axis runs over, the one named last changes fastest.
Arguments:
- quant_in: bfloat16 [4096, 7168], P('expert', 'dp'), may hold values from -4 to 4
- quant_scale: float32 [4096, 56], P('expert'), may hold values from 0.25 to 4
- grad_out: bfloat16 [4096, 7168], P('expert', 'dp'), may hold values from -6 to 6
- route_ids: int32 [4096, 1], replicated, may hold values from 0 to 31; in each aligned block of 128 rows (0 to 127, 128 to 255, ...) at most 12 rows name the same one
- route_weights: float32 [4096, 1], replicated, may hold values from 0.1 to 1
- w_gate: bfloat16 [32, 7168, 1024], P('expert', 'dp'), may hold values from -0.0625 to 0.0625
- w_up: bfloat16 [32, 7168, 1024], P('expert', 'dp'), may hold values from -0.0625 to 0.0625
- w_down: bfloat16 [32, 1024, 7168], P('expert', None, 'dp'), may hold values from -0.1875 to 0.1875
Outputs:
- grad_in: bfloat16 [4096, 7168], P('expert', 'dp')
- grad_gate: bfloat16 [32, 7168, 1024], P('expert', 'dp')
- grad_up: bfloat16 [32, 7168, 1024], P('expert', 'dp')
- grad_down: bfloat16 [32, 1024, 7168], P('expert', None, 'dp')
The draws below stay inside these ranges and needn't reach their ends.
Inputs may be any that keep to these rules, and one draw needn't show every extreme that they name: `route_ids`: each token names 1 different experts. Among the 128 tokens of one aligned group, no expert is named more than 12 times, a bound that some block reaches.
All inputs are finite; a program needn't handle non-finite values.
Results may differ from the reference program's by a relative error of at most 0.0076.
Values may be sent and summed in bfloat16 or wider, within the bound.
A program may use at most 64 MiB of HBM per device.

```python
import math
import jax
import jax.numpy as jnp
import numpy as np
from jax import lax

D = 7168
H = 1024
E = 32
K = 1
QB = 128
TOK_E = 128
CAP = 12
TOKENS = 4096


def block_scale(rng, extent, pieces, low, top_value):
    def one(axis_at, blocks):
        steps = jax.random.uniform(jax.random.fold_in(jax.random.fold_in(rng, 6), axis_at), (blocks,), jnp.float32, low / len(pieces), top_value / len(pieces))
        return jnp.repeat(jnp.exp(steps), extent[axis_at] // blocks).reshape((-1,) + (1,) * (len(extent) - axis_at - 1))

    loudness = one(*pieces[0])
    for cut in pieces[1:]:
        loudness = loudness * one(*cut)
    return loudness


def routed_block(stream_key, own, number, rows, count, top, reach, skew):
    sequence = jax.random.permutation(stream_key, count)
    crowded, usual = shares(count, rows * top, reach, skew, True), shares(count, rows * top, reach, skew, False)
    places = jnp.arange(count)

    def named(lengths, rotation):
        used = int((lengths > 0).sum())
        fixed = max(1, used // 4)
        moved = fixed + (places - fixed + rotation * (used - fixed)) % max(1, count - fixed)
        return jnp.zeros((count,), jnp.int32).at[sequence[jnp.where(places < fixed, places, moved)]].set(jnp.asarray(lengths, jnp.int32))

    lengths = jnp.where(number % 4 == 0, named(crowded, number // 4), named(usual, number - number // 4 - 1))
    mixed = jax.random.permutation(jax.random.fold_in(own, 3), count)
    source_of, sink = mixed[0:count // 2 * 2:2], mixed[1:count // 2 * 2:2]
    slack = jnp.minimum(lengths[source_of] - 1, reach - lengths[sink]) // 2
    slack = jnp.where((source_of == sequence[0]) | (sink == sequence[0]) | (lengths[sink] == 0), 0, jnp.maximum(slack, 0))
    moved = jax.random.randint(jax.random.fold_in(own, 4), (count // 2,), 0, 1 << 20) % (slack + 1)
    lengths = lengths.at[source_of].add(-moved).at[sink].add(moved)
    labels = jnp.searchsorted(jnp.cumsum(lengths), jnp.arange(rows * top), side="right").astype(jnp.int32)
    grid = labels.reshape(top, rows).T
    grid = grid[jax.random.permutation(jax.random.fold_in(own, 1), rows)]
    rotation = jax.random.randint(jax.random.fold_in(own, 2), (rows, 1), 0, top)
    return jnp.take_along_axis(grid, (jnp.arange(top)[None, :] + rotation) % top, axis=1)


def shares(amount, total, most, skew, full):
    weights = [(1 << 20) // math.isqrt(standing ** skew) + 1 for standing in range(1, amount + 1)]
    largest = most if full else min(most, max(-(-total // amount), total * weights[0] // sum(weights)))
    least = 1 if total - largest >= amount - 1 else 0
    holding, spare = [largest] + [least] * (amount - 1), total - largest - least * (amount - 1)
    while spare > 0:
        movable = [i for i in range(1, amount) if holding[i] < largest] or [i for i in range(1, amount) if holding[i] < most]
        mass, remaining = sum([weights[i] for i in movable]), spare
        for i in movable:
            more = min(most - holding[i], max(1, remaining * weights[i] // mass), spare)
            holding[i] = holding[i] + more
            spare = spare - more
    return np.array(holding)


def gaussian(rng, dims, spread, most, pieces=(), kind=jnp.bfloat16):
    gain = block_scale(rng, dims, pieces, -0.22, 0.18) if pieces else 1.0
    entries = jax.random.normal(rng, dims, jnp.float32) * spread * gain
    return jnp.minimum(jnp.maximum(entries, -most), most).astype(kind)


def setup_inputs(seed: int = 0) -> dict:
    arg_keys = jax.random.split(jax.random.key(seed), 9)
    quant_in = gaussian(arg_keys[0], (TOKENS, D), 1.0, 4.0, ((0, 32), (1, 32)))
    quant_scale = jnp.clip(jnp.exp(math.log(4.0) - 2.7725887 * jax.random.uniform(arg_keys[1], (TOKENS, D // QB), jnp.float32) ** block_scale(arg_keys[1], (TOKENS, D // QB), ((0, 32),), -0.2, 0.2)), 0.25, 4.0)
    grad_out = gaussian(arg_keys[2], (TOKENS, D), 1.0, 6.0, ((0, 32), (1, 32)))
    route_ids_keys = jax.random.split(jax.random.fold_in(arg_keys[3], 1), TOKENS // TOK_E)
    route_ids_turns = jax.random.permutation(jax.random.fold_in(arg_keys[3], 3), TOKENS // TOK_E)
    route_ids = jax.vmap(lambda own, number: routed_block(jax.random.fold_in(arg_keys[3], 2), own, number, TOK_E, E, K, CAP, 2))(route_ids_keys, route_ids_turns).reshape((TOKENS, K))
    route_weights = jnp.clip(jax.random.uniform(arg_keys[4], (TOKENS, K), jnp.float32, 0.1, 1.0), 0.1, 1.0)
    w_gate = gaussian(arg_keys[5], (E, D, H), D ** -0.5, 0.0625, ((0, 32), (1, 32)))
    w_up = gaussian(arg_keys[6], (E, D, H), D ** -0.5, 0.0625, ((0, 32), (1, 32)))
    w_down = gaussian(arg_keys[7], (E, H, D), H ** -0.5, 0.1875, ((0, 32), (2, 32)))
    return dict(quant_in=quant_in, quant_scale=quant_scale, grad_out=grad_out, route_ids=route_ids, route_weights=route_weights, w_gate=w_gate, w_up=w_up, w_down=w_down)


def slot_tables(route_rows, weights):
    expert_ids = jnp.arange(E, dtype=jnp.int32)
    matches = route_rows[:, :, None] == expert_ids[None, None, :]
    member = jnp.sum(matches.astype(jnp.int32), axis=1)
    chosen = jnp.sum(jnp.where(matches, weights[:, :, None], jnp.zeros_like(weights)[:, :, None]), axis=1)
    earlier = jnp.cumsum(member, axis=0) - member
    places = jnp.arange(CAP, dtype=jnp.int32)
    select = (member.T[:, None, :] == 1) & (earlier.T[:, None, :] == places[None, :, None])
    slot_weight = jnp.sum(jnp.where(select, chosen.T[:, None, :], jnp.zeros_like(chosen).T[:, None, :]), axis=2)
    return select, slot_weight


def gated_backward(summed):
    gate_sum = summed[..., 0, :]
    up_sum = summed[..., 1, :]
    down_sum = summed[..., 2, :]
    sigma = jax.nn.sigmoid(gate_sum)
    hidden = gate_sum * sigma * up_sum
    grad_gate_in = down_sum * up_sum * sigma * (1.0 + gate_sum * (1.0 - sigma))
    grad_up_in = down_sum * gate_sum * sigma
    return jnp.stack((hidden, grad_gate_in, grad_up_in), axis=-2).astype(jnp.bfloat16)


def reference(quant_in, quant_scale, grad_out, route_ids, route_weights, w_gate, w_up, w_down):
    token_count = quant_in.shape[0]
    groups = token_count // TOK_E
    scaled_in = quant_in.astype(jnp.float32).reshape(token_count, D // QB, QB) * quant_scale[:, :, None]
    rows_in = scaled_in.reshape(token_count, D).astype(jnp.bfloat16)
    select, slot_weight = jax.vmap(slot_tables)(route_ids.reshape(groups, TOK_E, K), route_weights.reshape(groups, TOK_E, K))
    pickers = select.astype(jnp.float32)
    rows_group = rows_in.astype(jnp.float32).reshape(groups, TOK_E, D)
    grads_group = grad_out.astype(jnp.float32).reshape(groups, TOK_E, D)

    def one_expert(expert_id):
        picked = lax.dynamic_index_in_dim(pickers, expert_id, 1, keepdims=False)
        rows_x = jnp.einsum("gct,gtd->gcd", picked, rows_group).astype(jnp.bfloat16).reshape(groups * CAP, D)
        rows_g = jnp.einsum("gct,gtd->gcd", picked, grads_group).astype(jnp.bfloat16).reshape(groups * CAP, D)
        slot_scale = lax.dynamic_index_in_dim(slot_weight, expert_id, 1, keepdims=False).reshape(groups * CAP)
        scaled = (slot_scale[:, None] * rows_g.astype(jnp.float32)).astype(jnp.bfloat16)
        gate_weight = lax.dynamic_index_in_dim(w_gate, expert_id, 0, keepdims=False)
        up_weight = lax.dynamic_index_in_dim(w_up, expert_id, 0, keepdims=False)
        down_weight = lax.dynamic_index_in_dim(w_down, expert_id, 0, keepdims=False)
        gate_sum = jnp.dot(rows_x, gate_weight, preferred_element_type=jnp.float32)
        up_sum = jnp.dot(rows_x, up_weight, preferred_element_type=jnp.float32)
        down_sum = jnp.dot(scaled, down_weight.T, preferred_element_type=jnp.float32)
        values = gated_backward(jnp.stack((gate_sum, up_sum, down_sum), axis=1))
        hidden = values[:, 0, :]
        grad_gate_in = values[:, 1, :]
        grad_up_in = values[:, 2, :]
        gate_grad = jnp.dot(rows_x.T, grad_gate_in, preferred_element_type=jnp.float32).astype(jnp.bfloat16)
        up_grad = jnp.dot(rows_x.T, grad_up_in, preferred_element_type=jnp.float32).astype(jnp.bfloat16)
        down_grad = jnp.dot(hidden.T, scaled, preferred_element_type=jnp.float32).astype(jnp.bfloat16)
        slot_grad = jnp.dot(grad_gate_in, gate_weight.T, preferred_element_type=jnp.float32)
        slot_grad = slot_grad + jnp.dot(grad_up_in, up_weight.T, preferred_element_type=jnp.float32)
        return gate_grad, up_grad, down_grad, slot_grad.astype(jnp.bfloat16).reshape(groups, CAP, D)

    grad_gate, grad_up, grad_down, slot_grads = lax.map(one_expert, jnp.arange(E, dtype=jnp.int32))
    summed_in = jnp.einsum("gect,egcd->gtd", pickers, slot_grads.astype(jnp.float32))
    grad_in = summed_in.reshape(token_count, D).astype(jnp.bfloat16)
    return grad_in, grad_gate, grad_up, grad_down
```

```python
import functools

import jax
import jax.numpy as jnp
from jax import lax
from jax.experimental import pallas as pl
from jax.experimental.pallas import tpu as pltpu
from jax.sharding import PartitionSpec as P

MESH = pl.DeviceIdType.MESH
F32 = jnp.float32
BF16 = jnp.bfloat16

D = 7168
H = 1024
QB = 128
TOK = 128
CAP = 12
Z = 32
SIDE = 4
W = 224
HALF = H // 2
SLOT = 16
WIDE = 384
ROWS = Z * CAP
TYPE = ROWS // 2
BLK = TYPE // SIDE
LANES = HALF // SIDE
GROUP = 8


def dot(a, b, dims=((1,), (0,))):
    return lax.dot_general(a, b, (dims, ((), ())), preferred_element_type=F32)


def iota(shape, dim):
    return lax.broadcasted_iota(jnp.int32, shape, dim)


def one_hot(cond):
    return jnp.where(cond, 1.0, 0.0).astype(BF16)


def hop(p):
    return 16 + ((p + 1) // 2) * (1 - 2 * (p % 2))


def to_column(row):
    diag = iota((TOK, TOK), 0) == iota((TOK, TOK), 1)
    spread = jnp.broadcast_to(row, (TOK, TOK))
    return jnp.sum(jnp.where(diag, spread, jnp.zeros_like(spread)), axis=1, keepdims=True)


def kernel(
    quant_ref, scale_ref, grad_ref, ids_ref, wts_ref, wg_hbm, wu_hbm, wd_hbm,
    gin_ref, gg_hbm, gu_hbm, gd_hbm,
    send, recv, recvp, pick, wg, wu, wd, wgp, wup, wdp, xo, xp, go, gp,
    part, rx1, sum1, rx2, val, rsend, rrecv, gg, gu, gd,
    zs, zr, fs, fr, ws, wr, wl, cs, cr, ps, pr, bs, br, os,
):
    z = lax.axis_index("expert")
    d = lax.axis_index("dp")
    cx, cy, core = d // 8, (d // 2) % 4, d % 2
    mate = {"dp": d + 1 - 2 * core}

    def at_x(j):
        return {"dp": (((cx + j) % 4) * 4 + cy) * 2 + core}

    def at_y(j):
        return {"dp": (cx * 4 + (cy + j) % 4) * 2 + core}

    def remote(src, dst, s, r, device):
        return pltpu.make_async_remote_copy(
            src_ref=src, dst_ref=dst, send_sem=s, recv_sem=r, device_id=device, device_id_type=MESH
        )

    barrier = pltpu.get_barrier_semaphore()

    def greet(k, carry):
        pl.semaphore_signal(
            barrier, inc=1, device_id={"expert": (z + k) % Z}, device_id_type=MESH
        )
        return carry

    lax.fori_loop(1, Z, greet, 0)
    for device in [mate] + [at_x(j) for j in (1, 2, 3)] + [at_y(j) for j in (1, 2, 3)]:
        pl.semaphore_signal(barrier, inc=1, device_id=device, device_id_type=MESH)

    local = [
        pltpu.make_async_copy(wg_hbm, wg, wl.at[0]),
        pltpu.make_async_copy(wu_hbm, wu, wl.at[1]),
        pltpu.make_async_copy(wd_hbm, wd, wl.at[2]),
    ]
    for c in local:
        c.start()

    ids = ids_ref[pl.ds(z, 1), :]
    member = one_hot(iota((Z, TOK), 0) == jnp.broadcast_to(ids, (Z, TOK)))
    before = one_hot(iota((TOK, TOK), 0) < iota((TOK, TOK), 1))
    earlier = dot(member, before)
    slot = jnp.sum(member.astype(F32) * earlier, axis=0, keepdims=True).astype(jnp.int32)
    k = (ids - z) & (Z - 1)
    place = SLOT * jnp.where(k < 16, 31 - 2 * k, 2 * k - 32)
    late = jnp.where(slot >= 6, 1, 0)
    rows = iota((Z * SLOT, TOK), 0)
    pick_main = one_hot(rows == jnp.broadcast_to(place + slot, (Z * SLOT, TOK)))
    pick_tail = one_hot(rows == jnp.broadcast_to(place + CAP + late, (Z * SLOT, TOK)))
    pick[...] = pick_main
    sixth = to_column(slot - 6 * late)
    weight = to_column(wts_ref[pl.ds(z, 1), :])

    picker = jnp.where(
        iota((D // QB, W), 0) == ((W * d + iota((D // QB, W), 1)) >> 7), 1.0, 0.0
    ).astype(F32)
    col_scale = jnp.dot(
        scale_ref[...], picker, precision=lax.Precision.HIGHEST, preferred_element_type=F32
    )
    x = (quant_ref[...].astype(F32) * col_scale).astype(BF16)
    g = (grad_ref[...].astype(F32) * weight).astype(BF16)
    r, c = iota((W, WIDE), 0), iota((W, WIDE), 1)
    put_x = one_hot(r == c)
    put_g = one_hot(((c >= 256) & (r == c - 256)) | ((c >= W) & (c < 256) & (r == c - 96)))
    put_t = one_hot(r == 160 + (c & 63))
    wide = (dot(x, put_x) + dot(g, put_g)).astype(BF16)
    tail = dot(g, put_t)
    tail = jnp.where((iota((TOK, WIDE), 1) >> 6) == sixth, tail, 0.0).astype(BF16)
    for q in range(4):
        at = pl.ds(128 * q, 128)
        send[at, :] = (
            dot(pick_main[128 * q : 128 * q + 128], wide)
            + dot(pick_tail[128 * q : 128 * q + 128], tail)
        ).astype(BF16)

    pl.semaphore_wait(barrier, Z - 1 + 7)

    def block(p):
        return pl.ds(pl.multiple_of(p * SLOT, SLOT), SLOT)

    def out_copy(p):
        return remote(
            send.at[block(p)], recv.at[block(p)], zs.at[p], zr.at[p],
            {"expert": (z + hop(p)) % Z},
        )

    def start_out(p, carry):
        out_copy(p).start()
        return carry

    lax.fori_loop(0, Z - 1, start_out, 0)
    recv[pl.ds((Z - 1) * SLOT, SLOT), :] = send[pl.ds((Z - 1) * SLOT, SLOT), :]

    other = pl.ds(pl.multiple_of((1 - core) * HALF, HALF), HALF)
    mine = pl.ds(pl.multiple_of(core * HALF, HALF), HALF)
    weights_out = [
        remote(wg_hbm.at[:, other], wgp, ws.at[0], wr.at[0], mate),
        remote(wu_hbm.at[:, other], wup, ws.at[1], wr.at[1], mate),
        remote(wd_hbm.at[other, :], wdp, ws.at[2], wr.at[2], mate),
    ]
    for c in weights_out:
        c.start()

    gr = GROUP * CAP
    i, j = iota((gr, 128), 0), iota((gr, 128), 1)
    src, cc = j >> 4, j & 15
    take_main = one_hot((cc < CAP) & (i == CAP * src + cc))
    off = i - CAP * src - 6 * (cc - CAP)
    take_tail = one_hot((cc >= CAP) & (cc < CAP + 2) & (off >= 0) & (off < 6))
    ri = iota((gr, WIDE), 0)
    tail_lane = (iota((gr, WIDE), 1) >> 6) == ri - 6 * ((ri * 43) >> 8)
    r, c = iota((WIDE, W), 0), iota((WIDE, W), 1)
    get_g = one_hot(((c < 128) & (r == c + 256)) | ((c >= 128) & (c < 160) & (r == c + 96)))
    get_t = one_hot((c >= 160) & (c - 160 == (r & 63)))

    def unpack(ref, q, x_ref, g_ref):
        raw = ref[pl.ds(128 * q, 128), :]
        main = dot(take_main, raw).astype(BF16)
        ends = jnp.where(tail_lane, dot(take_tail, raw), 0.0).astype(BF16)
        x_ref[pl.ds(gr * q, gr), :] = main[:, :W]
        g_ref[pl.ds(gr * q, gr), :] = (dot(main, get_g) + dot(ends, get_t)).astype(BF16)

    def forward_copy(q):
        at = pl.ds(128 * q, 128)
        return remote(recv.at[at], recvp.at[at], fs.at[q], fr.at[q], mate)

    def arrive(p, carry):
        out_copy(p).wait_recv()
        return carry

    first = (cx, cy)
    second = (cy, cx)
    peer1 = (at_x, at_y)
    peer2 = (at_y, at_x)

    def rows_of(t, a):
        return pl.ds(pl.multiple_of(TYPE * t + BLK * a, 16), BLK)

    def lanes_of(b):
        return pl.ds(pl.multiple_of(LANES * b, LANES), LANES)

    def rs1(t, j):
        a = (first[t] + j) % 4
        return remote(
            part.at[:, rows_of(t, a), :], rx1.at[t, j - 1], cs.at[0, t, j - 1], cr.at[0, t, j - 1],
            peer1[t](j),
        )

    def rs2(t, j):
        b = (second[t] + j) % 4
        return remote(
            sum1.at[t, :, :, lanes_of(b)], rx2.at[t, j - 1], cs.at[1, t, j - 1],
            cr.at[1, t, j - 1], peer2[t](j),
        )

    def ag2(t, j, back=0):
        ref = val.at[core, :, rows_of(t, first[t]), lanes_of((second[t] + 4 - back) % 4)]
        return remote(ref, ref, cs.at[2, t, j - 1], cr.at[2, t, j - 1], peer2[t](j))

    def ag1(t, j, back=0):
        ref = val.at[core, :, rows_of(t, (first[t] + 4 - back) % 4), :]
        return remote(ref, ref, cs.at[3, t, j - 1], cr.at[3, t, j - 1], peer1[t](j))

    def pair(t, half):
        ref = val.at[half, :, pl.ds(TYPE * t, TYPE), :]
        return remote(ref, ref, ps.at[t], pr.at[t], mate)

    peers = (1, 2, 3)

    def products(t):
        at = pl.ds(TYPE * t, TYPE)
        nt = ((1,), (1,))
        a, b = xo[at, :], xp[at, :]
        part[0, at, :] = (dot(a, wg[:, mine]) + dot(b, wgp[...])).astype(BF16)
        part[1, at, :] = (dot(a, wu[:, mine]) + dot(b, wup[...])).astype(BF16)
        a, b = go[at, :], gp[at, :]
        part[2, at, :] = (dot(a, wd[mine, :], nt) + dot(b, wdp[...], nt)).astype(BF16)

    for t in (0, 1):
        for q in (2 * t, 2 * t + 1):
            lax.fori_loop(GROUP * q, min(GROUP * q + GROUP, Z - 1), arrive, 0)
            forward_copy(q).start()
        if t == 0:
            for c in local:
                c.wait()
            for c in weights_out:
                c.wait_recv()
        for q in (2 * t, 2 * t + 1):
            unpack(recv, q, xo, go)
            forward_copy(q).wait_recv()
            unpack(recvp, q, xp, gp)
        products(t)
        for j in peers:
            rs1(t, j).start()

    for t in (0, 1):
        for j in peers:
            rs1(t, j).wait_recv()
        total = part[:, rows_of(t, first[t]), :].astype(F32)
        for j in peers:
            total = total + rx1[t, j - 1].astype(F32)
        sum1[t] = total.astype(BF16)
        for j in peers:
            rs2(t, j).start()

    for t in (0, 1):
        for j in peers:
            rs2(t, j).wait_recv()
        total = sum1[t, :, :, lanes_of(second[t])].astype(F32)
        for j in peers:
            total = total + rx2[t, j - 1].astype(F32)
        gate, up, down = total[0], total[1], total[2]
        sigma = jax.nn.sigmoid(gate)
        at, lanes = rows_of(t, first[t]), lanes_of(second[t])
        val[core, 0, at, lanes] = (gate * sigma * up).astype(BF16)
        val[core, 1, at, lanes] = (
            down * up * sigma * (1.0 + gate * (1.0 - sigma))
        ).astype(BF16)
        val[core, 2, at, lanes] = (down * gate * sigma).astype(BF16)
        for j in peers:
            ag2(t, j).start()

    for t in (0, 1):
        for j in peers:
            ag2(t, j, j).wait_recv()
        for j in peers:
            ag1(t, j).start()

    for t in (0, 1):
        for j in peers:
            ag1(t, j, j).wait_recv()
        pair(t, core).start()

    i, j = iota((128, gr), 0), iota((128, gr), 1)
    spread = one_hot(((i & 15) < CAP) & (j == CAP * (i >> 4) + (i & 15)))

    def back_copy(p):
        return remote(
            rsend.at[block(p)], rrecv.at[block(p)], bs.at[p], br.at[p],
            {"expert": (z + Z - hop(p)) % Z},
        )

    def start_back(p, carry):
        back_copy(p).start()
        return carry

    nt = ((1,), (1,))
    for t in (0, 1):
        pair(t, 1 - core).wait_recv()
        at = pl.ds(TYPE * t, TYPE)
        slots = (
            dot(val[0, 1, at, :], wg[:, :HALF], nt)
            + dot(val[1, 1, at, :], wg[:, HALF:], nt)
            + dot(val[0, 2, at, :], wu[:, :HALF], nt)
            + dot(val[1, 2, at, :], wu[:, HALF:], nt)
        ).astype(BF16)
        for q in (0, 1):
            rsend[pl.ds(256 * t + 128 * q, 128), :] = dot(
                spread, slots[gr * q : gr * q + gr]
            ).astype(BF16)
        lax.fori_loop(16 * t, min(16 * t + 16, Z - 1), start_back, 0)
    rrecv[pl.ds((Z - 1) * SLOT, SLOT), :] = rsend[pl.ds((Z - 1) * SLOT, SLOT), :]

    tn = ((0,), (0,))
    for h in (0, 1):
        at = pl.ds(HALF * h, HALF)
        gg[:, at] = dot(xo[...], val[h, 1], tn).astype(BF16)
        gu[:, at] = dot(xo[...], val[h, 2], tn).astype(BF16)
        gd[at, :] = dot(val[h, 0], go[...], tn).astype(BF16)
    outs = [
        pltpu.make_async_copy(gg, gg_hbm, os.at[0]),
        pltpu.make_async_copy(gu, gu_hbm, os.at[1]),
        pltpu.make_async_copy(gd, gd_hbm, os.at[2]),
    ]
    for c in outs:
        c.start()

    def home(p, carry):
        back_copy(p).wait_recv()
        return carry

    lax.fori_loop(0, Z - 1, home, 0)
    gin_ref[...] = dot(pick[...], rrecv[...], tn).astype(BF16)

    def drain(p, carry):
        out_copy(p).wait_send()
        back_copy(p).wait_send()
        return carry

    lax.fori_loop(0, Z - 1, drain, 0)
    for c in weights_out:
        c.wait_send()
    for q in range(4):
        forward_copy(q).wait_send()
    for t in (0, 1):
        pair(t, core).wait_send()
        for j in peers:
            rs1(t, j).wait_send()
            rs2(t, j).wait_send()
            ag2(t, j).wait_send()
            ag1(t, j).wait_send()
    for c in outs:
        c.wait()


def on_device(quant_in, quant_scale, grad_out, route_ids, route_weights, w_gate, w_up, w_down):
    vmem = pl.BlockSpec(memory_space=pltpu.VMEM)
    hbm = pl.BlockSpec(memory_space=pl.ANY)
    dma = pltpu.SemaphoreType.DMA
    shapes = [
        ((Z * SLOT, WIDE), BF16), ((Z * SLOT, WIDE), BF16), ((Z * SLOT, WIDE), BF16),
        ((Z * SLOT, TOK), BF16),
        ((W, H), BF16), ((W, H), BF16), ((H, W), BF16),
        ((W, HALF), BF16), ((W, HALF), BF16), ((HALF, W), BF16),
        ((ROWS, W), BF16), ((ROWS, W), BF16), ((ROWS, W), BF16), ((ROWS, W), BF16),
        ((3, ROWS, HALF), BF16),
        ((2, 3, 3, BLK, HALF), BF16), ((2, 3, BLK, HALF), BF16), ((2, 3, 3, BLK, LANES), BF16),
        ((2, 3, ROWS, HALF), BF16),
        ((Z * SLOT, W), BF16), ((Z * SLOT, W), BF16),
        ((W, H), BF16), ((W, H), BF16), ((H, W), BF16),
    ]
    sems = [
        (Z - 1,), (Z - 1,), (4,), (4,), (3,), (3,), (3,), (4, 2, 3), (4, 2, 3), (2,), (2,),
        (Z - 1,), (Z - 1,), (3,),
    ]
    out_shape = [
        jax.ShapeDtypeStruct((TOK, W), BF16),
        jax.ShapeDtypeStruct((W, H), BF16),
        jax.ShapeDtypeStruct((W, H), BF16),
        jax.ShapeDtypeStruct((H, W), BF16),
    ]
    gin, gg, gu, gd = pl.pallas_call(
        kernel,
        out_shape=out_shape,
        in_specs=[vmem] * 5 + [hbm] * 3,
        out_specs=[vmem] + [hbm] * 3,
        scratch_shapes=[pltpu.VMEM(s, t) for s, t in shapes] + [dma(s) for s in sems],
        compiler_params=pltpu.CompilerParams(
            collective_id=0, has_side_effects=True, vmem_limit_bytes=48 * 1024 * 1024
        ),
        cost_estimate=pl.CostEstimate(
            flops=2 * 8 * ROWS * W * H, bytes_accessed=12 * W * H, transcendentals=ROWS * H // 32
        ),
    )(
        quant_in, quant_scale, grad_out,
        route_ids.reshape(Z, TOK), route_weights.reshape(Z, TOK),
        w_gate[0], w_up[0], w_down[0],
    )
    return gin, gg[None], gu[None], gd[None]


def solution(mesh):
    placed = (
        P("expert", "dp"),
        P("expert", None),
        P("expert", "dp"),
        P(),
        P(),
        P("expert", "dp", None),
        P("expert", "dp", None),
        P("expert", None, "dp"),
    )
    return jax.shard_map(
        on_device,
        mesh=mesh,
        in_specs=placed,
        out_specs=(
            P("expert", "dp"),
            P("expert", "dp", None),
            P("expert", "dp", None),
            P("expert", None, "dp"),
        ),
        check_vma=False,
    )
```

```python
import functools

import jax
import jax.numpy as jnp
from jax import lax
from jax.experimental import pallas as pl
from jax.experimental.pallas import tpu as pltpu
from jax.sharding import PartitionSpec as P

MESH = pl.DeviceIdType.MESH
F32 = jnp.float32
BF16 = jnp.bfloat16

D = 7168
H = 1024
QB = 128
TOK = 128
CAP = 12
Z = 32
SIDE = 4
W = 224
HALF = H // 2
SLOT = 16
WIDE = 384
ROWS = Z * CAP
CHUNKS = 4
GROUP = Z // CHUNKS
CROWS = GROUP * CAP
BLK = CROWS // SIDE
LANES = HALF // SIDE
MINE = CROWS // 2
TN = ((0,), (0,))
VMEM = 63 * 1024 * 1024


def dot(a, b, dims=((1,), (0,))):
    return lax.dot_general(a, b, (dims, ((), ())), preferred_element_type=F32)


def iota(shape, dim):
    return lax.broadcasted_iota(jnp.int32, shape, dim)


def one_hot(cond):
    return jnp.where(cond, 1.0, 0.0).astype(BF16)


def hop(p):
    return 16 + ((p + 1) // 2) * (1 - 2 * (p % 2))


def to_column(row):
    diag = iota((TOK, TOK), 0) == iota((TOK, TOK), 1)
    spread = jnp.broadcast_to(row, (TOK, TOK))
    return jnp.sum(jnp.where(diag, spread, jnp.zeros_like(spread)), axis=1, keepdims=True)


def sixths(i):
    return i - 6 * ((i * 43) >> 8)


def kernel(
    quant_ref, scale_ref, grad_ref, ids_ref, wts_ref, wg_hbm, wu_hbm, wd_hbm,
    gin_ref, gg_hbm, gu_hbm, gd_hbm,
    gg, gu, gd, send, recv, recvp, wg, wu, wd, wgp, wup, wdp, mg, mu, xo, xp, go, gp,
    part, rx1, sum1, rx2, vals, val, slotp, rslot, rsend, rb,
    zs, zr, fs, fr, ws, wr, wl, cs, cr, ms, mr, ps, pr, bs, br, hs, hr, os,
):
    z = lax.axis_index("expert")
    d = lax.axis_index("dp")
    cx, cy, core = d // 8, (d // 2) % 4, d % 2
    mate = {"dp": d + 1 - 2 * core}

    def at_x(j):
        return {"dp": (((cx + j) % 4) * 4 + cy) * 2 + core}

    def at_y(j):
        return {"dp": (cx * 4 + (cy + j) % 4) * 2 + core}

    def remote(src, dst, s, r, device):
        return pltpu.make_async_remote_copy(
            src_ref=src, dst_ref=dst, send_sem=s, recv_sem=r, device_id=device, device_id_type=MESH
        )

    barrier = pltpu.get_barrier_semaphore()

    def greet(k, carry):
        pl.semaphore_signal(
            barrier, inc=1, device_id={"expert": (z + k) % Z}, device_id_type=MESH
        )
        return carry

    lax.fori_loop(1, Z, greet, 0)
    for device in [mate] + [at_x(j) for j in (1, 2, 3)] + [at_y(j) for j in (1, 2, 3)]:
        pl.semaphore_signal(barrier, inc=1, device_id=device, device_id_type=MESH)

    local = [
        pltpu.make_async_copy(wg_hbm, wg, wl.at[0]),
        pltpu.make_async_copy(wu_hbm, wu, wl.at[1]),
        pltpu.make_async_copy(wd_hbm, wd, wl.at[2]),
    ]
    for c in local:
        c.start()

    ids = ids_ref[pl.ds(z, 1), :]
    member = one_hot(iota((Z, TOK), 0) == jnp.broadcast_to(ids, (Z, TOK)))
    before = one_hot(iota((TOK, TOK), 0) < iota((TOK, TOK), 1))
    earlier = dot(member, before)
    slot = jnp.sum(member.astype(F32) * earlier, axis=0, keepdims=True).astype(jnp.int32)
    k = (ids - z) & (Z - 1)
    p = jnp.where(k < 16, 31 - 2 * k, 2 * k - 32)
    late = jnp.where(slot >= 6, 1, 0)
    sixth = slot - 6 * late
    rows = iota((Z * SLOT, TOK), 0)

    def pickers(base):
        return (
            one_hot(rows == jnp.broadcast_to(base + slot, (Z * SLOT, TOK))),
            one_hot(rows == jnp.broadcast_to(base + CAP + late, (Z * SLOT, TOK))),
        )

    pick_main, pick_tail = pickers(SLOT * p)
    weight = wts_ref[pl.ds(z, 1), :]

    picker = jnp.where(
        iota((W, D // QB), 1) == ((W * d + iota((W, D // QB), 0)) >> 7), 1.0, 0.0
    ).astype(F32)
    col_scale = jnp.dot(
        picker, scale_ref[...], precision=lax.Precision.HIGHEST, preferred_element_type=F32
    )
    x = (quant_ref[...].astype(F32) * col_scale).astype(BF16)
    g = (grad_ref[...].astype(F32) * weight).astype(BF16)
    r, c = iota((W, WIDE), 0), iota((W, WIDE), 1)
    put_x = one_hot(r == c)
    put_g = one_hot(((c >= 256) & (r == c - 256)) | ((c >= W) & (c < 256) & (r == c - 96)))
    put_t = one_hot(r == 160 + (c & 63))
    wide = (dot(x, put_x, TN) + dot(g, put_g, TN)).astype(BF16)
    tail = dot(g, put_t, TN)
    tail = jnp.where((iota((TOK, WIDE), 1) >> 6) == to_column(sixth), tail, 0.0).astype(BF16)
    for q in range(CHUNKS):
        send[pl.ds(128 * q, 128), :] = (
            dot(pick_main[128 * q : 128 * q + 128], wide)
            + dot(pick_tail[128 * q : 128 * q + 128], tail)
        ).astype(BF16)

    pl.semaphore_wait(barrier, Z - 1 + 7)

    def block(q):
        return pl.ds(pl.multiple_of(q * SLOT, SLOT), SLOT)

    def out_copy(q):
        return remote(
            send.at[block(q)], recv.at[block(q)], zs.at[q], zr.at[q],
            {"expert": (z + hop(q)) % Z},
        )

    def start_out(q, carry):
        out_copy(q).start()
        return carry

    lax.fori_loop(0, Z - 1, start_out, 0)
    recv[pl.ds((Z - 1) * SLOT, SLOT), :] = send[pl.ds((Z - 1) * SLOT, SLOT), :]

    other = pl.ds(pl.multiple_of((1 - core) * HALF, HALF), HALF)
    mine = pl.ds(pl.multiple_of(core * HALF, HALF), HALF)
    weights_out = [
        remote(wg.at[:, other], wgp, ws.at[0], wr.at[0], mate),
        remote(wu.at[:, other], wup, ws.at[1], wr.at[1], mate),
        remote(wd.at[:, other], wdp, ws.at[2], wr.at[2], mate),
    ]
    for c in local:
        c.wait()
    for c in weights_out:
        c.start()

    i, j = iota((CROWS, 128), 0), iota((CROWS, 128), 1)
    src, cc = j >> 4, j & 15
    take_main = one_hot((cc < CAP) & (i == CAP * src + cc))
    off = i - CAP * src - 6 * (cc - CAP)
    take_tail = one_hot((cc >= CAP) & (cc < CAP + 2) & (off >= 0) & (off < 6))
    tail_lane = (iota((CROWS, WIDE), 1) >> 6) == sixths(iota((CROWS, WIDE), 0))
    r, c = iota((WIDE, W), 0), iota((WIDE, W), 1)
    get_g = one_hot(((c < 128) & (r == c + 256)) | ((c >= 128) & (c < 160) & (r == c + 96)))
    get_t = one_hot((c >= 160) & (c - 160 == (r & 63)))

    i, j = iota((4 * SLOT, MINE), 0), iota((4 * SLOT, MINE), 1)
    src, cc = i >> 4, i & 15
    lay_main = one_hot((cc < CAP) & (j == CAP * src + cc))
    off = j - CAP * src - 6 * (cc - CAP)
    lay_tail = one_hot((cc >= CAP) & (cc < CAP + 2) & (off >= 0) & (off < 6))
    lay_lane = (iota((MINE, WIDE), 1) >> 6) == sixths(iota((MINE, WIDE), 0))
    repeat = one_hot(iota((64, WIDE), 0) == (iota((64, WIDE), 1) & 63))

    second_core = core.astype(F32)
    r, c = iota((W, HALF), 0), iota((W, HALF), 1)
    lane0 = jnp.where(r == c, 1.0, 0.0)
    lane1 = jnp.where(
        ((c >= W) & (c < 256) & (r == c - 96))
        | ((c >= 256) & (c < WIDE) & (r == c - 256))
        | ((c >= WIDE) & (c < WIDE + 64) & (r == c - W)),
        1.0,
        0.0,
    )
    lane_own = (lane0 + second_core * (lane1 - lane0)).astype(BF16)
    lane_mate = (lane1 + second_core * (lane0 - lane1)).astype(BF16)
    for c in weights_out:
        c.wait_recv()
    mg[...] = (dot(wg[:, mine], lane_own, TN) + dot(wgp[...], lane_mate, TN)).astype(BF16)
    mu[...] = (dot(wu[:, mine], lane_own, TN) + dot(wup[...], lane_mate, TN)).astype(BF16)

    apart = ((p >> 2) + core) & 1
    back_main, back_tail = pickers(SLOT * (16 * apart + 4 * (p >> 3) + (p & 3)))

    first = (cx, cy, cx, cy)
    second = (cy, cx, cy, cx)
    peer1 = (at_x, at_y, at_x, at_y)
    peer2 = (at_y, at_x, at_y, at_x)
    peers = (1, 2, 3)

    def rows_of(t):
        return pl.ds(CROWS * t, CROWS)

    def lanes_of(a):
        return pl.ds(pl.multiple_of(LANES * a, LANES), LANES)

    def blk_of(b):
        return pl.ds(pl.multiple_of(BLK * b, 8), BLK)

    def forward_copy(t):
        at = pl.ds(128 * t, 128)
        return remote(recv.at[at], recvp.at[at], fs.at[t], fr.at[t], mate)

    def rs1(t, j):
        return remote(
            part.at[:, rows_of(t), lanes_of((first[t] + j) % 4)], rx1.at[t, j - 1],
            cs.at[0, t, j - 1], cr.at[0, t, j - 1], peer1[t](j),
        )

    def rs2(t, j):
        return remote(
            sum1.at[t, :, blk_of((second[t] + j) % 4), :], rx2.at[t, j - 1],
            cs.at[1, t, j - 1], cr.at[1, t, j - 1], peer2[t](j),
        )

    def ag2(t, j, back=0):
        ref = vals.at[t, (second[t] + 4 - back) % 4]
        return remote(ref, ref, cs.at[2, t, j - 1], cr.at[2, t, j - 1], peer2[t](j))

    def ag1(t, j, back=0):
        ref = val.at[core, :, rows_of(t), lanes_of((first[t] + 4 - back) % 4)]
        return remote(ref, ref, cs.at[3, t, j - 1], cr.at[3, t, j - 1], peer1[t](j))

    def half_copy(t):
        at = pl.ds(pl.multiple_of(CROWS * t + MINE * (1 - core), 16), MINE)
        return remote(slotp.at[at, :], rslot.at[t], ms.at[t], mr.at[t], mate)

    def pair(t, half):
        ref = val.at[half, :, rows_of(t), :]
        return remote(ref, ref, ps.at[t], pr.at[t], mate)

    def back_copy(u):
        return remote(
            rsend.at[block(u)], rb.at[block(u)], bs.at[u], br.at[u],
            {"expert": (z + Z - hop(8 * (u // 4) + 4 * core + u % 4)) % Z},
        )

    def home_copy(t):
        return remote(
            rb.at[pl.ds(64 * t, 64)], rb.at[pl.ds(256 + 64 * t, 64)], hs.at[t], hr.at[t], mate
        )

    def each(first_one, last_one, act):
        def step(q, carry):
            act(q)
            return carry

        lax.fori_loop(first_one, last_one, step, 0)

    def unpack(ref, t, x_ref, g_ref):
        raw = ref[pl.ds(128 * t, 128), :]
        main = dot(take_main, raw).astype(BF16)
        ends = jnp.where(tail_lane, dot(take_tail, raw), 0.0).astype(BF16)
        x_ref[rows_of(t), :] = main[:, :W]
        g_ref[rows_of(t), :] = (dot(main, get_g) + dot(ends, get_t)).astype(BF16)

    def arrive(t):
        each(GROUP * t, min(GROUP * t + GROUP, Z - 1), lambda q: out_copy(q).wait_recv())
        forward_copy(t).start()

    def products(t):
        at = rows_of(t)
        unpack(recv, t, xo, go)
        forward_copy(t).wait_recv()
        unpack(recvp, t, xp, gp)
        a, b = xo[at, :], xp[at, :]
        part[0, at, :] = (dot(a, wg[:, mine]) + dot(b, wgp[...])).astype(BF16)
        part[1, at, :] = (dot(a, wu[:, mine]) + dot(b, wup[...])).astype(BF16)
        a, b = go[at, :], gp[at, :]
        part[2, at, :] = (dot(a, wd[:, mine]) + dot(b, wdp[...])).astype(BF16)
        for j in peers:
            rs1(t, j).start()

    def add_first(t):
        for j in peers:
            rs1(t, j).wait_recv()
        total = part[:, rows_of(t), lanes_of(first[t])].astype(F32)
        for j in peers:
            total = total + rx1[t, j - 1].astype(F32)
        sum1[t] = total
        for j in peers:
            rs2(t, j).start()

    def gated(t):
        for j in peers:
            rs2(t, j).wait_recv()
        total = sum1[t, :, blk_of(second[t]), :]
        for j in peers:
            total = total + rx2[t, j - 1]
        gate, up, down = total[0], total[1], total[2]
        sigma = jax.nn.sigmoid(gate)
        vals[t, second[t], 0] = gate * sigma * up
        vals[t, second[t], 1] = down * up * sigma * (1.0 + gate * (1.0 - sigma))
        vals[t, second[t], 2] = down * gate * sigma
        for j in peers:
            ag2(t, j).start()

    def gather(t):
        for j in peers:
            ag2(t, j, j).wait_recv()
        for kind in range(3):
            val[core, kind, rows_of(t), lanes_of(first[t])] = jnp.concatenate(
                [vals[t, b, kind] for b in range(SIDE)], axis=0
            ).astype(BF16)
        for j in peers:
            ag1(t, j).start()

    def slots(t):
        for j in peers:
            ag1(t, j, j).wait_recv()
        at = rows_of(t)
        slotp[at, :] = dot(val[core, 1, at, :], mg[...]) + dot(val[core, 2, at, :], mu[...])
        half_copy(t).start()
        pair(t, core).start()

    def give_back(t):
        half_copy(t).wait_recv()
        at = pl.ds(pl.multiple_of(CROWS * t + MINE * core, 16), MINE)
        total = (slotp[at, :] + rslot[t]).astype(BF16)
        ends = jnp.where(lay_lane, dot(total[:, WIDE : WIDE + 64], repeat), 0.0).astype(BF16)
        rsend[pl.ds(64 * t, 64), :] = (
            dot(lay_main, total[:, :WIDE]) + dot(lay_tail, ends)
        ).astype(BF16)
        last = 4 * t + 4 if t < CHUNKS - 1 else 4 * t + 4 - core
        each(4 * t, last, lambda u: back_copy(u).start())

    def come_home(t):
        last = 4 * t + 4 if t < CHUNKS - 1 else 4 * t + 4 - core
        each(4 * t, last, lambda u: back_copy(u).wait_recv())
        home_copy(t).start()

    plan = (
        (arrive, 0), (products, 0), (add_first, 0), (arrive, 1), (products, 1), (gated, 0),
        (arrive, 2), (gather, 0), (products, 2), (arrive, 3), (add_first, 1), (products, 3),
        (slots, 0), (gated, 1), (give_back, 0), (add_first, 2), (add_first, 3), (gather, 1),
        (gated, 2), (gated, 3), (slots, 1), (gather, 2), (give_back, 1), (gather, 3),
        (slots, 2), (give_back, 2), (slots, 3), (give_back, 3),
    )
    for act, t in plan:
        act(t)

    @pl.when(core == 1)
    def _():
        rb[pl.ds(240, SLOT), :] = rsend[pl.ds(240, SLOT), :]

    for t in range(CHUNKS):
        pair(t, 1 - core).wait_recv()
    outs = []
    for t, (ref, out, rows_in, kind) in enumerate(
        ((gg, gg_hbm, xo, 1), (gu, gu_hbm, xo, 2), (gd, gd_hbm, go, 0))
    ):
        come_home(t)
        for h in (0, 1):
            ref[:, pl.ds(HALF * h, HALF)] = dot(rows_in[...], val[h, kind], TN).astype(BF16)
        outs.append(pltpu.make_async_copy(ref, out, os.at[t]))
        outs[t].start()
    come_home(CHUNKS - 1)

    r, c = iota((W, WIDE), 0), iota((W, WIDE), 1)
    lane0 = jnp.where(r == c, 1.0, 0.0)
    lane1 = jnp.where(
        ((r < 128) & (c == r + 256)) | ((r >= 128) & (r < 160) & (c == r + 96)), 1.0, 0.0
    )
    lane2 = jnp.where((r >= 160) & (r - 160 == (c & 63)), 1.0, 0.0)
    from_main = (lane0 + second_core * (lane1 - lane0)).astype(BF16)
    from_tail = (second_core * lane2).astype(BF16)
    for t in range(CHUNKS):
        home_copy(t).wait_recv()
    landed = rb[...]
    main = dot(landed, back_main, TN).astype(BF16)
    ends = jnp.where(
        (iota((WIDE, TOK), 0) >> 6) == jnp.broadcast_to(sixth, (WIDE, TOK)),
        dot(landed, back_tail, TN),
        0.0,
    ).astype(BF16)
    gin_ref[...] = (dot(from_main, main) + dot(from_tail, ends)).astype(BF16)

    each(0, Z - 1, lambda q: out_copy(q).wait_send())
    each(0, 16 - core, lambda u: back_copy(u).wait_send())
    for c in outs:
        c.wait()
    for c in weights_out:
        c.wait_send()
    for t in range(CHUNKS):
        forward_copy(t).wait_send()
        half_copy(t).wait_send()
        pair(t, core).wait_send()
        home_copy(t).wait_send()
        for j in peers:
            rs1(t, j).wait_send()
            rs2(t, j).wait_send()
            ag2(t, j).wait_send()
            ag1(t, j).wait_send()


def copy_out(a, b, c, d, oa, ob, oc, od, sa, sb, sc, sd, come, go):
    held = (sa, sb, sc, sd)
    ins = [pltpu.make_async_copy(r, v, come.at[n]) for n, (r, v) in enumerate(zip((a, b, c, d), held))]
    outs = [pltpu.make_async_copy(v, r, go.at[n]) for n, (v, r) in enumerate(zip(held, (oa, ob, oc, od)))]
    for one in ins:
        one.start()
    for one, two in zip(ins, outs):
        one.wait()
        two.start()
    for two in outs:
        two.wait()


def on_device(quant_in, quant_scale, grad_out, route_ids, route_weights, w_gate, w_up, w_down):
    vmem = pl.BlockSpec(memory_space=pltpu.VMEM)
    anywhere = pl.BlockSpec(memory_space=pl.ANY)
    dma = pltpu.SemaphoreType.DMA
    half = ((W, HALF), BF16)
    whole = ((W, H), BF16)
    packed = ((Z * SLOT, WIDE), BF16)
    dense = ((ROWS, W), BF16)
    shapes = [
        whole, whole, whole, packed, packed, packed, whole, whole, whole, half, half, half,
        ((HALF, HALF), BF16), ((HALF, HALF), BF16), dense, dense, dense, dense,
        ((3, ROWS, HALF), BF16), ((CHUNKS, 3, 3, CROWS, LANES), BF16),
        ((CHUNKS, 3, CROWS, LANES), F32), ((CHUNKS, 3, 3, BLK, LANES), F32),
        ((CHUNKS, SIDE, 3, BLK, LANES), F32), ((2, 3, ROWS, HALF), BF16),
        ((ROWS, HALF), F32), ((CHUNKS, MINE, HALF), F32),
        ((Z * SLOT // 2, WIDE), BF16), packed,
    ]
    four = (CHUNKS,)
    sems = [
        (Z - 1,), (Z - 1,), four, four, (3,), (3,), (3,), (4, CHUNKS, 3), (4, CHUNKS, 3),
        four, four, four, four, (16,), (16,), four, four, (3,),
    ]
    out_shape = [
        jax.ShapeDtypeStruct((W, TOK), BF16),
        jax.ShapeDtypeStruct((W, H), BF16),
        jax.ShapeDtypeStruct((W, H), BF16),
        jax.ShapeDtypeStruct((W, H), BF16),
    ]
    results = pl.pallas_call(
        kernel,
        out_shape=out_shape,
        in_specs=[vmem] * 5 + [anywhere] * 3,
        out_specs=[vmem] + [anywhere] * 3,
        scratch_shapes=[pltpu.VMEM(s, t) for s, t in shapes] + [dma(s) for s in sems],
        compiler_params=pltpu.CompilerParams(
            collective_id=0, has_side_effects=True, vmem_limit_bytes=VMEM
        ),
        cost_estimate=pl.CostEstimate(
            flops=2 * 8 * ROWS * W * H, bytes_accessed=12 * W * H, transcendentals=ROWS * H // 32
        ),
    )(
        quant_in.T, quant_scale.T, grad_out.T,
        route_ids.reshape(Z, TOK), route_weights.reshape(Z, TOK),
        w_gate[0], w_up[0], w_down[0].T,
    )
    gin, gg, gu, gd = pl.pallas_call(
        copy_out,
        out_shape=out_shape,
        in_specs=[anywhere] * 4,
        out_specs=[anywhere] * 4,
        scratch_shapes=[pltpu.VMEM(o.shape, BF16) for o in out_shape] + [dma((4,)), dma((4,))],
        compiler_params=pltpu.CompilerParams(vmem_limit_bytes=VMEM),
        cost_estimate=pl.CostEstimate(flops=0, bytes_accessed=14 * W * H, transcendentals=0),
    )(*results)
    return gin.T, gg[None], gu[None], gd.T[None]


def solution(mesh):
    placed = (
        P("expert", "dp"),
        P("expert", None),
        P("expert", "dp"),
        P(),
        P(),
        P("expert", "dp", None),
        P("expert", "dp", None),
        P("expert", None, "dp"),
    )
    return jax.shard_map(
        on_device,
        mesh=mesh,
        in_specs=placed,
        out_specs=(
            P("expert", "dp"),
            P("expert", "dp", None),
            P("expert", "dp", None),
            P("expert", None, "dp"),
        ),
        check_vma=False,
    )
```

```python
import functools

import jax
import jax.numpy as jnp
from jax import lax
from jax.experimental import pallas as pl
from jax.experimental.pallas import tpu as pltpu
from jax.sharding import PartitionSpec as P

MESH = pl.DeviceIdType.MESH
F32 = jnp.float32
BF16 = jnp.bfloat16

D = 7168
H = 1024
QB = 128
TOK = 128
CAP = 12
Z = 32
SIDE = 4
W = 224
HALF = H // 2
SLOT = 16
WIDE = 384
ROWS = Z * CAP
CHUNKS = 4
GROUP = Z // CHUNKS
CROWS = GROUP * CAP
BLK = CROWS // SIDE
LANES = HALF // SIDE
MINE = CROWS // 2
TN = ((0,), (0,))
VMEM = 63 * 1024 * 1024


def dot(a, b, dims=((1,), (0,))):
    return lax.dot_general(a, b, (dims, ((), ())), preferred_element_type=F32)


def iota(shape, dim):
    return lax.broadcasted_iota(jnp.int32, shape, dim)


def one_hot(cond):
    return jnp.where(cond, 1.0, 0.0).astype(BF16)


def hop(p):
    return 16 + ((p + 1) // 2) * (1 - 2 * (p % 2))


def to_column(row):
    diag = iota((TOK, TOK), 0) == iota((TOK, TOK), 1)
    spread = jnp.broadcast_to(row, (TOK, TOK))
    return jnp.sum(jnp.where(diag, spread, jnp.zeros_like(spread)), axis=1, keepdims=True)


def sixths(i):
    return i - 6 * ((i * 43) >> 8)


def kernel(
    quant_hbm, scale_hbm, grad_hbm, ids_hbm, wts_hbm, wg_hbm, wu_hbm, wd_hbm,
    gin_ref, gg_hbm, gu_hbm, gd_hbm,
    quant_ref, scale_ref, grad_ref, ids_ref, wts_ref, gg, gu, gd, send, recv, recvp, wg, wu, wd, wgp, wup, wdp, mg, mu, xo, xp, go, gp,
    part, rx1, sum1, rx2, vals, val, slotp, rslot, rsend, rb,
    zs, zr, fs, fr, ws, wr, wl, cs, cr, ms, mr, ps, pr, bs, br, hs, hr, os, es,
):
    z = lax.axis_index("expert")
    d = lax.axis_index("dp")
    cx, cy, core = d // 8, (d // 2) % 4, d % 2
    mate = {"dp": d + 1 - 2 * core}

    def at_x(j):
        return {"dp": (((cx + j) % 4) * 4 + cy) * 2 + core}

    def at_y(j):
        return {"dp": (cx * 4 + (cy + j) % 4) * 2 + core}

    def remote(src, dst, s, r, device):
        return pltpu.make_async_remote_copy(
            src_ref=src, dst_ref=dst, send_sem=s, recv_sem=r, device_id=device, device_id_type=MESH
        )

    barrier = pltpu.get_barrier_semaphore()

    def greet(k, carry):
        pl.semaphore_signal(
            barrier, inc=1, device_id={"expert": (z + k) % Z}, device_id_type=MESH
        )
        return carry

    lax.fori_loop(1, Z, greet, 0)
    for device in [mate] + [at_x(j) for j in (1, 2, 3)] + [at_y(j) for j in (1, 2, 3)]:
        pl.semaphore_signal(barrier, inc=1, device_id=device, device_id_type=MESH)

    early = [
        pltpu.make_async_copy(a, b, es.at[n])
        for n, (a, b) in enumerate(
            (
                (ids_hbm, ids_ref), (wts_hbm, wts_ref), (scale_hbm, scale_ref),
                (quant_hbm, quant_ref), (grad_hbm, grad_ref),
            )
        )
    ]
    for c in early:
        c.start()
    local = [
        pltpu.make_async_copy(wg_hbm, wg, wl.at[0]),
        pltpu.make_async_copy(wu_hbm, wu, wl.at[1]),
        pltpu.make_async_copy(wd_hbm, wd, wl.at[2]),
    ]
    for c in local:
        c.start()

    for c in early:
        c.wait()
    ids = ids_ref[pl.ds(z, 1), :]
    member = one_hot(iota((Z, TOK), 0) == jnp.broadcast_to(ids, (Z, TOK)))
    before = one_hot(iota((TOK, TOK), 0) < iota((TOK, TOK), 1))
    earlier = dot(member, before)
    slot = jnp.sum(member.astype(F32) * earlier, axis=0, keepdims=True).astype(jnp.int32)
    k = (ids - z) & (Z - 1)
    p = jnp.where(k < 16, 31 - 2 * k, 2 * k - 32)
    late = jnp.where(slot >= 6, 1, 0)
    sixth = slot - 6 * late
    rows = iota((Z * SLOT, TOK), 0)

    def pickers(base):
        return (
            one_hot(rows == jnp.broadcast_to(base + slot, (Z * SLOT, TOK))),
            one_hot(rows == jnp.broadcast_to(base + CAP + late, (Z * SLOT, TOK))),
        )

    pick_main, pick_tail = pickers(SLOT * p)
    weight = wts_ref[pl.ds(z, 1), :]

    picker = jnp.where(
        iota((W, D // QB), 1) == ((W * d + iota((W, D // QB), 0)) >> 7), 1.0, 0.0
    ).astype(F32)
    col_scale = jnp.dot(
        picker, scale_ref[...], precision=lax.Precision.HIGHEST, preferred_element_type=F32
    )
    x = (quant_ref[...].astype(F32) * col_scale).astype(BF16)
    g = (grad_ref[...].astype(F32) * weight).astype(BF16)
    r, c = iota((W, WIDE), 0), iota((W, WIDE), 1)
    put_x = one_hot(r == c)
    put_g = one_hot(((c >= 256) & (r == c - 256)) | ((c >= W) & (c < 256) & (r == c - 96)))
    put_t = one_hot(r == 160 + (c & 63))
    wide = (dot(x, put_x, TN) + dot(g, put_g, TN)).astype(BF16)
    tail = dot(g, put_t, TN)
    tail = jnp.where((iota((TOK, WIDE), 1) >> 6) == to_column(sixth), tail, 0.0).astype(BF16)
    for q in range(CHUNKS):
        send[pl.ds(128 * q, 128), :] = (
            dot(pick_main[128 * q : 128 * q + 128], wide)
            + dot(pick_tail[128 * q : 128 * q + 128], tail)
        ).astype(BF16)

    pl.semaphore_wait(barrier, Z - 1 + 7)

    def block(q):
        return pl.ds(pl.multiple_of(q * SLOT, SLOT), SLOT)

    def out_copy(q):
        return remote(
            send.at[block(q)], recv.at[block(q)], zs.at[q], zr.at[q],
            {"expert": (z + hop(q)) % Z},
        )

    def start_out(q, carry):
        out_copy(q).start()
        return carry

    lax.fori_loop(0, Z - 1, start_out, 0)
    recv[pl.ds((Z - 1) * SLOT, SLOT), :] = send[pl.ds((Z - 1) * SLOT, SLOT), :]

    other = pl.ds(pl.multiple_of((1 - core) * HALF, HALF), HALF)
    mine = pl.ds(pl.multiple_of(core * HALF, HALF), HALF)
    weights_out = [
        remote(wg.at[:, other], wgp, ws.at[0], wr.at[0], mate),
        remote(wu.at[:, other], wup, ws.at[1], wr.at[1], mate),
        remote(wd.at[:, other], wdp, ws.at[2], wr.at[2], mate),
    ]
    for c in local:
        c.wait()
    for c in weights_out:
        c.start()

    i, j = iota((CROWS, 128), 0), iota((CROWS, 128), 1)
    src, cc = j >> 4, j & 15
    take_main = one_hot((cc < CAP) & (i == CAP * src + cc))
    off = i - CAP * src - 6 * (cc - CAP)
    take_tail = one_hot((cc >= CAP) & (cc < CAP + 2) & (off >= 0) & (off < 6))
    tail_lane = (iota((CROWS, WIDE), 1) >> 6) == sixths(iota((CROWS, WIDE), 0))
    r, c = iota((WIDE, W), 0), iota((WIDE, W), 1)
    get_g = one_hot(((c < 128) & (r == c + 256)) | ((c >= 128) & (c < 160) & (r == c + 96)))
    get_t = one_hot((c >= 160) & (c - 160 == (r & 63)))

    i, j = iota((4 * SLOT, MINE), 0), iota((4 * SLOT, MINE), 1)
    src, cc = i >> 4, i & 15
    lay_main = one_hot((cc < CAP) & (j == CAP * src + cc))
    off = j - CAP * src - 6 * (cc - CAP)
    lay_tail = one_hot((cc >= CAP) & (cc < CAP + 2) & (off >= 0) & (off < 6))
    lay_lane = (iota((MINE, WIDE), 1) >> 6) == sixths(iota((MINE, WIDE), 0))
    repeat = one_hot(iota((64, WIDE), 0) == (iota((64, WIDE), 1) & 63))

    second_core = core.astype(F32)
    r, c = iota((W, HALF), 0), iota((W, HALF), 1)
    lane0 = jnp.where(r == c, 1.0, 0.0)
    lane1 = jnp.where(
        ((c >= W) & (c < 256) & (r == c - 96))
        | ((c >= 256) & (c < WIDE) & (r == c - 256))
        | ((c >= WIDE) & (c < WIDE + 64) & (r == c - W)),
        1.0,
        0.0,
    )
    lane_own = (lane0 + second_core * (lane1 - lane0)).astype(BF16)
    lane_mate = (lane1 + second_core * (lane0 - lane1)).astype(BF16)
    for c in weights_out:
        c.wait_recv()
    mg[...] = (dot(wg[:, mine], lane_own, TN) + dot(wgp[...], lane_mate, TN)).astype(BF16)
    mu[...] = (dot(wu[:, mine], lane_own, TN) + dot(wup[...], lane_mate, TN)).astype(BF16)

    apart = ((p >> 2) + core) & 1
    back_main, back_tail = pickers(SLOT * (16 * apart + 4 * (p >> 3) + (p & 3)))

    first = (cx, cy, cx, cy)
    second = (cy, cx, cy, cx)
    peer1 = (at_x, at_y, at_x, at_y)
    peer2 = (at_y, at_x, at_y, at_x)
    peers = (1, 2, 3)

    def rows_of(t):
        return pl.ds(CROWS * t, CROWS)

    def lanes_of(a):
        return pl.ds(pl.multiple_of(LANES * a, LANES), LANES)

    def blk_of(b):
        return pl.ds(pl.multiple_of(BLK * b, 8), BLK)

    def forward_copy(t):
        at = pl.ds(128 * t, 128)
        return remote(recv.at[at], recvp.at[at], fs.at[t], fr.at[t], mate)

    def rs1(t, j):
        return remote(
            part.at[:, rows_of(t), lanes_of((first[t] + j) % 4)], rx1.at[t, j - 1],
            cs.at[0, t, j - 1], cr.at[0, t, j - 1], peer1[t](j),
        )

    def rs2(t, j):
        return remote(
            sum1.at[t, :, blk_of((second[t] + j) % 4), :], rx2.at[t, j - 1],
            cs.at[1, t, j - 1], cr.at[1, t, j - 1], peer2[t](j),
        )

    def ag2(t, j, back=0):
        ref = vals.at[t, (second[t] + 4 - back) % 4]
        return remote(ref, ref, cs.at[2, t, j - 1], cr.at[2, t, j - 1], peer2[t](j))

    def ag1(t, j, back=0):
        ref = val.at[core, :, rows_of(t), lanes_of((first[t] + 4 - back) % 4)]
        return remote(ref, ref, cs.at[3, t, j - 1], cr.at[3, t, j - 1], peer1[t](j))

    def half_copy(t):
        at = pl.ds(pl.multiple_of(CROWS * t + MINE * (1 - core), 16), MINE)
        return remote(slotp.at[at, :], rslot.at[t], ms.at[t], mr.at[t], mate)

    def pair(t, half):
        ref = val.at[half, :, rows_of(t), :]
        return remote(ref, ref, ps.at[t], pr.at[t], mate)

    def back_copy(u):
        return remote(
            rsend.at[block(u)], rb.at[block(u)], bs.at[u], br.at[u],
            {"expert": (z + Z - hop(8 * (u // 4) + 4 * core + u % 4)) % Z},
        )

    def home_copy(t):
        return remote(
            rb.at[pl.ds(64 * t, 64)], rb.at[pl.ds(256 + 64 * t, 64)], hs.at[t], hr.at[t], mate
        )

    def each(first_one, last_one, act):
        def step(q, carry):
            act(q)
            return carry

        lax.fori_loop(first_one, last_one, step, 0)

    def unpack(ref, t, x_ref, g_ref):
        raw = ref[pl.ds(128 * t, 128), :]
        main = dot(take_main, raw).astype(BF16)
        ends = jnp.where(tail_lane, dot(take_tail, raw), 0.0).astype(BF16)
        x_ref[rows_of(t), :] = main[:, :W]
        g_ref[rows_of(t), :] = (dot(main, get_g) + dot(ends, get_t)).astype(BF16)

    def arrive(t):
        each(GROUP * t, min(GROUP * t + GROUP, Z - 1), lambda q: out_copy(q).wait_recv())
        forward_copy(t).start()

    def products(t):
        at = rows_of(t)
        unpack(recv, t, xo, go)
        forward_copy(t).wait_recv()
        unpack(recvp, t, xp, gp)
        a, b = xo[at, :], xp[at, :]
        part[0, at, :] = (dot(a, wg[:, mine]) + dot(b, wgp[...])).astype(BF16)
        part[1, at, :] = (dot(a, wu[:, mine]) + dot(b, wup[...])).astype(BF16)
        a, b = go[at, :], gp[at, :]
        part[2, at, :] = (dot(a, wd[:, mine]) + dot(b, wdp[...])).astype(BF16)
        for j in peers:
            rs1(t, j).start()

    def add_first(t):
        for j in peers:
            rs1(t, j).wait_recv()
        total = part[:, rows_of(t), lanes_of(first[t])].astype(F32)
        for j in peers:
            total = total + rx1[t, j - 1].astype(F32)
        sum1[t] = total
        for j in peers:
            rs2(t, j).start()

    def gated(t):
        for j in peers:
            rs2(t, j).wait_recv()
        total = sum1[t, :, blk_of(second[t]), :]
        for j in peers:
            total = total + rx2[t, j - 1]
        gate, up, down = total[0], total[1], total[2]
        sigma = jax.nn.sigmoid(gate)
        vals[t, second[t], 0] = gate * sigma * up
        vals[t, second[t], 1] = down * up * sigma * (1.0 + gate * (1.0 - sigma))
        vals[t, second[t], 2] = down * gate * sigma
        for j in peers:
            ag2(t, j).start()

    def gather(t):
        for j in peers:
            ag2(t, j, j).wait_recv()
        for kind in range(3):
            val[core, kind, rows_of(t), lanes_of(first[t])] = jnp.concatenate(
                [vals[t, b, kind] for b in range(SIDE)], axis=0
            ).astype(BF16)
        for j in peers:
            ag1(t, j).start()

    def slots(t):
        for j in peers:
            ag1(t, j, j).wait_recv()
        at = rows_of(t)
        slotp[at, :] = dot(val[core, 1, at, :], mg[...]) + dot(val[core, 2, at, :], mu[...])
        half_copy(t).start()
        pair(t, core).start()

    def give_back(t):
        half_copy(t).wait_recv()
        at = pl.ds(pl.multiple_of(CROWS * t + MINE * core, 16), MINE)
        total = (slotp[at, :] + rslot[t]).astype(BF16)
        ends = jnp.where(lay_lane, dot(total[:, WIDE : WIDE + 64], repeat), 0.0).astype(BF16)
        rsend[pl.ds(64 * t, 64), :] = (
            dot(lay_main, total[:, :WIDE]) + dot(lay_tail, ends)
        ).astype(BF16)
        last = 4 * t + 4 if t < CHUNKS - 1 else 4 * t + 4 - core
        each(4 * t, last, lambda u: back_copy(u).start())

    def come_home(t):
        last = 4 * t + 4 if t < CHUNKS - 1 else 4 * t + 4 - core
        each(4 * t, last, lambda u: back_copy(u).wait_recv())
        home_copy(t).start()

    plan = (
        (arrive, 0), (products, 0), (add_first, 0), (arrive, 1), (products, 1), (gated, 0),
        (arrive, 2), (gather, 0), (products, 2), (arrive, 3), (add_first, 1), (products, 3),
        (slots, 0), (gated, 1), (give_back, 0), (add_first, 2), (add_first, 3), (gather, 1),
        (gated, 2), (gated, 3), (slots, 1), (gather, 2), (give_back, 1), (gather, 3),
        (slots, 2), (give_back, 2), (slots, 3), (give_back, 3),
    )
    for act, t in plan:
        act(t)

    @pl.when(core == 1)
    def _():
        rb[pl.ds(240, SLOT), :] = rsend[pl.ds(240, SLOT), :]

    for t in range(CHUNKS):
        pair(t, 1 - core).wait_recv()
    outs = []
    for t, (ref, out, rows_in, kind) in enumerate(
        ((gg, gg_hbm, xo, 1), (gu, gu_hbm, xo, 2), (gd, gd_hbm, go, 0))
    ):
        come_home(t)
        for h in (0, 1):
            ref[:, pl.ds(HALF * h, HALF)] = dot(rows_in[...], val[h, kind], TN).astype(BF16)
        outs.append(pltpu.make_async_copy(ref, out, os.at[t]))
        outs[t].start()
    come_home(CHUNKS - 1)

    r, c = iota((W, WIDE), 0), iota((W, WIDE), 1)
    lane0 = jnp.where(r == c, 1.0, 0.0)
    lane1 = jnp.where(
        ((r < 128) & (c == r + 256)) | ((r >= 128) & (r < 160) & (c == r + 96)), 1.0, 0.0
    )
    lane2 = jnp.where((r >= 160) & (r - 160 == (c & 63)), 1.0, 0.0)
    from_main = (lane0 + second_core * (lane1 - lane0)).astype(BF16)
    from_tail = (second_core * lane2).astype(BF16)
    for t in range(CHUNKS):
        home_copy(t).wait_recv()
    landed = rb[...]
    main = dot(landed, back_main, TN).astype(BF16)
    ends = jnp.where(
        (iota((WIDE, TOK), 0) >> 6) == jnp.broadcast_to(sixth, (WIDE, TOK)),
        dot(landed, back_tail, TN),
        0.0,
    ).astype(BF16)
    gin_ref[...] = (dot(from_main, main) + dot(from_tail, ends)).astype(BF16)

    each(0, Z - 1, lambda q: out_copy(q).wait_send())
    each(0, 16 - core, lambda u: back_copy(u).wait_send())
    for c in outs:
        c.wait()
    for c in weights_out:
        c.wait_send()
    for t in range(CHUNKS):
        forward_copy(t).wait_send()
        half_copy(t).wait_send()
        pair(t, core).wait_send()
        home_copy(t).wait_send()
        for j in peers:
            rs1(t, j).wait_send()
            rs2(t, j).wait_send()
            ag2(t, j).wait_send()
            ag1(t, j).wait_send()


def copy_out(a, b, c, d, oa, ob, oc, od, sa, sb, sc, sd, come, go):
    held = (sa, sb, sc, sd)
    ins = [pltpu.make_async_copy(r, v, come.at[n]) for n, (r, v) in enumerate(zip((a, b, c, d), held))]
    outs = [pltpu.make_async_copy(v, r, go.at[n]) for n, (v, r) in enumerate(zip(held, (oa, ob, oc, od)))]
    for one in ins:
        one.start()
    for one, two in zip(ins, outs):
        one.wait()
        two.start()
    for two in outs:
        two.wait()


def on_device(quant_in, quant_scale, grad_out, route_ids, route_weights, w_gate, w_up, w_down):
    vmem = pl.BlockSpec(memory_space=pltpu.VMEM)
    anywhere = pl.BlockSpec(memory_space=pl.ANY)
    dma = pltpu.SemaphoreType.DMA
    half = ((W, HALF), BF16)
    whole = ((W, H), BF16)
    packed = ((Z * SLOT, WIDE), BF16)
    dense = ((ROWS, W), BF16)
    wide_first = ((W, TOK), BF16)
    shapes = [
        wide_first, ((D // QB, TOK), F32), wide_first, ((Z, TOK), jnp.int32), ((Z, TOK), F32),
        whole, whole, whole, packed, packed, packed, whole, whole, whole, half, half, half,
        ((HALF, HALF), BF16), ((HALF, HALF), BF16), dense, dense, dense, dense,
        ((3, ROWS, HALF), BF16), ((CHUNKS, 3, 3, CROWS, LANES), BF16),
        ((CHUNKS, 3, CROWS, LANES), F32), ((CHUNKS, 3, 3, BLK, LANES), F32),
        ((CHUNKS, SIDE, 3, BLK, LANES), F32), ((2, 3, ROWS, HALF), BF16),
        ((ROWS, HALF), F32), ((CHUNKS, MINE, HALF), F32),
        ((Z * SLOT // 2, WIDE), BF16), packed,
    ]
    four = (CHUNKS,)
    sems = [
        (Z - 1,), (Z - 1,), four, four, (3,), (3,), (3,), (4, CHUNKS, 3), (4, CHUNKS, 3),
        four, four, four, four, (16,), (16,), four, four, (3,), (5,),
    ]
    out_shape = [
        jax.ShapeDtypeStruct((W, TOK), BF16),
        jax.ShapeDtypeStruct((W, H), BF16),
        jax.ShapeDtypeStruct((W, H), BF16),
        jax.ShapeDtypeStruct((W, H), BF16),
    ]
    results = pl.pallas_call(
        kernel,
        out_shape=out_shape,
        in_specs=[anywhere] * 8,
        out_specs=[vmem] + [anywhere] * 3,
        scratch_shapes=[pltpu.VMEM(s, t) for s, t in shapes] + [dma(s) for s in sems],
        compiler_params=pltpu.CompilerParams(
            collective_id=0, has_side_effects=True, vmem_limit_bytes=VMEM
        ),
        cost_estimate=pl.CostEstimate(
            flops=2 * 8 * ROWS * W * H, bytes_accessed=12 * W * H, transcendentals=ROWS * H // 32
        ),
    )(
        quant_in.T, quant_scale.T, grad_out.T,
        route_ids.reshape(Z, TOK), route_weights.reshape(Z, TOK),
        w_gate[0], w_up[0], w_down[0].T,
    )
    gin, gg, gu, gd = pl.pallas_call(
        copy_out,
        out_shape=out_shape,
        in_specs=[anywhere] * 4,
        out_specs=[anywhere] * 4,
        scratch_shapes=[pltpu.VMEM(o.shape, BF16) for o in out_shape] + [dma((4,)), dma((4,))],
        compiler_params=pltpu.CompilerParams(vmem_limit_bytes=VMEM),
        cost_estimate=pl.CostEstimate(flops=0, bytes_accessed=14 * W * H, transcendentals=0),
    )(*results)
    return gin.T, gg[None], gu[None], gd.T[None]


def solution(mesh):
    placed = (
        P("expert", "dp"),
        P("expert", None),
        P("expert", "dp"),
        P(),
        P(),
        P("expert", "dp", None),
        P("expert", "dp", None),
        P("expert", None, "dp"),
    )
    return jax.shard_map(
        on_device,
        mesh=mesh,
        in_specs=placed,
        out_specs=(
            P("expert", "dp"),
            P("expert", "dp", None),
            P("expert", "dp", None),
            P("expert", None, "dp"),
        ),
        check_vma=False,
    )
```
